1024 devices in a mesh: dp: 16 (over z_lo, y), fsdp: 64 (over x, z_hi, core).
Axes of the slice: x: 8, y: 8, z: 8 (z_hi: 4, z_lo: 2; z = z_hi * 2 + z_lo), core: 2. Of those that a mesh axis runs over, the one named last changes fastest.
Arguments:
- patches: bfloat16 [147456, 6144], P(('dp', 'fsdp')), may hold values from -6 to 6
- labels: int32 [147456], P(('dp', 'fsdp')), may hold values from 0 to 149
- weight: bfloat16 [6144, 150], P('fsdp'), may hold values from -0.21875 to 0.21875
- gain: bfloat16 [6144], P('fsdp'), may hold values from 0.099609375 to 1.8984375
- counts: int32 [4096], P(('dp', 'fsdp')), may hold values from 1 to 36, as said below
- plan: int32 [1024, 2], P(('dp', 'fsdp')), may hold values from 0 to 3, as said below
Outputs:
- logits: bfloat16 [147456, 150], P(('dp', 'fsdp'))
- input_grad: bfloat16 [147456, 6144], P(('dp', 'fsdp'))
- weight_grad: float32 [6144, 150], P('fsdp')
- gain_grad: float32 [6144], P('fsdp')
The draws below stay inside these ranges and needn't reach their ends.
Inputs may be any that keep to these rules, and one draw needn't show every extreme that they name: `counts`: rows of an image slot at positions from its count on are padding. `plan`: per device, column 0 is the slot whose image goes to the next data group and column 1 the slot whose image goes to the previous one, groups wrapping around; the two columns differ.
All inputs are finite; a program needn't handle non-finite values.
Results may differ from the reference program's by a relative error of at most 0.017.
Values may be sent and summed in bfloat16 or wider, within the bound.
No kernel may reach another device: no remote copies, remote signals or barrier semaphores. Data moves between devices by JAX's collectives and lax.ppermute only.
A program may use at most 64 MiB of HBM per device.

```python
import math
import jax
import jax.numpy as jnp
from jax import lax

D = 6144
CLASSES = 150
IMG_DEV = 4
PATCH = 36
IMAGES = 4096
ROWS = 147456
N_DP = 16
N_FSDP = 64


def draw_counts(key, part):
    key = jax.random.fold_in(key, 11)
    first, second = jax.random.split(key)
    base = jax.random.randint(first, (IMAGES,), 1, PATCH + 1)
    full = jax.random.randint(second, (IMAGES,), 0, 4) == 0
    return jnp.where(full, PATCH, base).astype(jnp.int32)


def draw_plan(key, part):
    key = jax.random.fold_in(key, 23)
    first, second = jax.random.split(key)
    devices = N_DP * N_FSDP
    upward = jax.random.randint(first, (devices,), 0, IMG_DEV)
    offset = jax.random.randint(second, (devices,), 1, IMG_DEV)
    downward = (upward + offset) % IMG_DEV
    return jnp.stack([upward, downward], axis=1).astype(jnp.int32)


def with_ends(entries, own_key, smallest, top_value):
    extent = entries.shape
    index_at = [jax.random.randint(jax.random.fold_in(own_key, axis), (), 0, extent[axis]) for axis in range(len(extent))]
    entries = entries.at[tuple(index_at)].set(smallest)
    longest = extent.index(max(extent))
    index_at[longest] = (index_at[longest] + 1) % extent[longest]
    return entries.at[tuple(index_at)].set(top_value)


def level_of(stream_key, dims, cuts, smallest, top_value):
    factor_of, own = 1.0, jax.random.fold_in(stream_key, 6)
    for dim, parts in cuts:
        steps = jnp.exp(jax.random.uniform(jax.random.fold_in(own, dim), (parts,), jnp.float32, smallest / len(cuts), top_value / len(cuts)))
        factor_of = factor_of * jnp.repeat(steps, dims[dim] // parts).reshape([-1 if axis == dim else 1 for axis in range(len(dims))])
    return factor_of


def normal_values(key, shape, scale, limit, cuts=(), kind=jnp.bfloat16):
    loudness = level_of(key, shape, cuts, -0.22, 0.18) if cuts else 1.0
    entries = jax.random.normal(key, shape, jnp.float32) * scale * loudness
    return jnp.minimum(jnp.maximum(entries, -limit), limit).astype(kind)


def setup_inputs(seed: int = 0) -> dict:
    arg_keys = jax.random.split(jax.random.key(seed), 7)
    patches = normal_values(arg_keys[0], (ROWS, D), 1.0, 6.0, ((0, 1024),))
    labels = with_ends(jax.random.randint(arg_keys[1], (ROWS,), 0, CLASSES), jax.random.fold_in(arg_keys[1], 1), 0, CLASSES - 1).astype(jnp.int32)
    weight = normal_values(arg_keys[2], (D, CLASSES), (D // 9) ** -0.5, 0.21875, ((0, 64),))
    gain = jnp.clip(1.0 + 0.18 * jax.random.normal(arg_keys[3], (D,), jnp.float32), 0.099609375, 1.8984375).astype(jnp.bfloat16)
    counts = draw_counts(jax.random.fold_in(arg_keys[6], 71), 0)
    plan = draw_plan(jax.random.fold_in(arg_keys[6], 71), 0)
    return {"patches": patches, "labels": labels, "weight": weight, "gain": gain, "counts": counts, "plan": plan}


def norm_forward(rows32):
    average = lax.optimization_barrier(jnp.mean(rows32, axis=1, keepdims=True))
    centred = rows32 - average
    inverse = lax.rsqrt(lax.optimization_barrier(jnp.mean(centred * centred, axis=1, keepdims=True)) + 1e-06)
    return (centred * inverse, inverse)

def norm_backward(dact, normed, inverse, gain32):
    dnorm = dact * gain32
    first = lax.optimization_barrier(jnp.mean(dnorm, axis=1, keepdims=True))
    second = lax.optimization_barrier(jnp.mean(dnorm * normed, axis=1, keepdims=True))
    return inverse * (dnorm - first - normed * second)

def reference(patches, labels, weight, gain, counts, plan):
    groups = N_DP
    shards = N_FSDP
    images = patches.reshape(groups, shards, IMG_DEV, PATCH, D)
    lengths = counts.reshape(groups, shards, IMG_DEV)
    routes = plan.reshape(groups, shards, 2)
    tags = labels.reshape(groups, shards * IMG_DEV * PATCH)
    slot_ids = jnp.arange(IMG_DEV, dtype=jnp.int32)
    places = jnp.arange(PATCH, dtype=jnp.int32)
    classes = jnp.arange(CLASSES, dtype=jnp.int32)
    gain32 = gain.astype(jnp.float32)

    def step(carry, group):
        upper = (group + 1) % groups
        lower = (group + groups - 1) % groups
        own = images[group]
        pick_up = routes[upper][:, 1]
        pick_low = routes[lower][:, 0]
        mine = routes[group]
        arrive_up = jnp.take_along_axis(images[upper], pick_up[:, None, None, None], axis=1)
        arrive_low = jnp.take_along_axis(images[lower], pick_low[:, None, None, None], axis=1)
        len_up = jnp.take_along_axis(lengths[upper], pick_up[:, None], axis=1)
        len_low = jnp.take_along_axis(lengths[lower], pick_low[:, None], axis=1)
        to_upper = slot_ids[None, :] == mine[:, 0:1]
        to_lower = slot_ids[None, :] == mine[:, 1:2]
        moved = jnp.where(to_upper[:, :, None, None], arrive_up, jnp.where(to_lower[:, :, None, None], arrive_low, own))
        live = jnp.where(to_upper, len_up, jnp.where(to_lower, len_low, lengths[group]))
        mask = (places[None, None, :] < live[:, :, None]).astype(jnp.float32).reshape(-1, 1)
        rows32 = moved.reshape(-1, D).astype(jnp.float32)
        normed, inverse = norm_forward(rows32)
        act = (normed * gain32).astype(jnp.bfloat16)
        pre = jnp.dot(act, weight, preferred_element_type=jnp.float32)
        shown = (pre * mask).astype(jnp.bfloat16)
        expo = jnp.exp(pre)
        prob = expo / lax.optimization_barrier(jnp.sum(expo, axis=1, keepdims=True))
        onehot = (tags[group][:, None] == classes[None, :]).astype(jnp.float32)
        dpre = (16.0 * (prob - onehot) * mask).astype(jnp.bfloat16)
        wterm = lax.dot_general(act, dpre, (((0,), (0,)), ((), ())), preferred_element_type=jnp.float32)
        dact = lax.dot_general(dpre, weight, (((1,), (1,)), ((), ())), preferred_element_type=jnp.float32)
        gterm = lax.optimization_barrier(jnp.sum(dact * normed, axis=0))
        grads = norm_backward(dact, normed, inverse, gain32).astype(jnp.bfloat16)
        return ((carry[0] + wterm, carry[1] + gterm), (shown, grads))
    start = (jnp.zeros((D, CLASSES), jnp.float32), jnp.zeros((D,), jnp.float32))
    sums, outs = lax.scan(step, start, jnp.arange(groups, dtype=jnp.int32))
    factor = 1.0 / math.sqrt(ROWS)
    logits = outs[0].reshape(ROWS, CLASSES)
    input_grad = outs[1].reshape(ROWS, D)
    return (logits, input_grad, sums[0] * factor, sums[1] * factor)
```

```python
import math

import jax
import jax.numpy as jnp
from jax import lax
from jax.sharding import Mesh
from jax.sharding import PartitionSpec as P

Z_LO, Y, X, Z_HI, CORE = 2, 8, 8, 4, 2
NAMES = ("z_lo", "y", "x", "z_hi", "core")
DATA = ("z_lo", "y")
PLANE = ("x", "z_hi")
CUBE = ("z_lo", "x", "z_hi")
PAD = 160


def from_behind(value, axes, steps):
    count = lax.axis_size(axes)
    pairs = [(source, (source + steps) % count) for source in range(count)]
    return lax.ppermute(value, axes, pairs)


def send_to_all(value, axes):
    count = lax.axis_size(axes)
    copies = jnp.broadcast_to(value[None], (count,) + value.shape)
    return lax.all_to_all(copies, axes, 0, 0)


def move(patches, counts, plan):
    total_rows, width = patches.shape
    slot_count = counts.shape[0]
    patch = total_rows // slot_count
    images = patches.reshape(slot_count, patch, width)
    up, down = plan[0, 0], plan[0, 1]

    def parcel(slot):
        image = lax.dynamic_index_in_dim(images, slot, 0, keepdims=False)
        count = lax.dynamic_slice_in_dim(counts, slot, 1).astype(jnp.bfloat16)
        return jnp.concatenate([image, jnp.broadcast_to(count[:, None], (1, width))])

    arrive_low = from_behind(parcel(up), DATA, 1)
    arrive_up = from_behind(parcel(down), DATA, -1)
    slot_ids = jnp.arange(slot_count, dtype=jnp.int32)
    to_upper = slot_ids == up
    to_lower = slot_ids == down
    moved = jnp.where(
        to_upper[:, None, None],
        arrive_up[None, :patch],
        jnp.where(to_lower[:, None, None], arrive_low[None, :patch], images),
    )
    live = jnp.where(
        to_upper,
        arrive_up[patch, 0].astype(jnp.int32),
        jnp.where(to_lower, arrive_low[patch, 0].astype(jnp.int32), counts),
    )
    places = jnp.arange(patch, dtype=jnp.int32)
    mask = (places[None, :] < live[:, None]).astype(jnp.float32).reshape(-1, 1)
    return moved.reshape(-1, width), mask


def body(patches, labels, weight, gain, counts, plan):
    total_rows, width = patches.shape
    share, classes = weight.shape
    gain32 = gain.astype(jnp.float32)[:, None]
    scaled = (weight.astype(jnp.float32) * gain32).astype(jnp.bfloat16)
    scaled = jnp.pad(scaled.T, ((0, PAD - classes), (0, 0)))
    rows, mask = move(patches, counts, plan)
    plane = send_to_all(scaled, PLANE)
    both = lax.all_gather(plane, "core")
    full = both.transpose(2, 1, 0, 3).reshape(PAD, width)

    rows32 = rows.astype(jnp.float32)
    average = jnp.mean(rows32, axis=1, keepdims=True)
    centred = rows32 - average
    inverse = lax.rsqrt(jnp.mean(centred * centred, axis=1, keepdims=True) + 1e-06)
    normed = centred * inverse
    act = normed.astype(jnp.bfloat16)
    pre = lax.dot_general(act, full, (((1,), (1,)), ((), ())), preferred_element_type=jnp.float32)
    class_ids = jnp.arange(PAD, dtype=jnp.int32)[None, :]
    expo = jnp.where(class_ids < classes, jnp.exp(pre), 0.0)
    prob = expo / jnp.sum(expo, axis=1, keepdims=True)
    onehot = (labels[:, None] == class_ids).astype(jnp.float32)
    dpre = (16.0 * (prob - onehot) * mask).astype(jnp.bfloat16)
    shown = (pre * mask)[:, :classes].astype(jnp.bfloat16)

    term = lax.dot_general(dpre, act, (((0,), (0,)), ((), ())), preferred_element_type=jnp.float32)
    blocks = term.astype(jnp.bfloat16).reshape(Z_LO, PAD // Z_LO, X, Z_HI, CORE, share)
    blocks = blocks.transpose(4, 0, 2, 3, 1, 5).reshape(CORE, Z_LO * X * Z_HI, PAD // Z_LO, share)
    core = lax.axis_index("core")
    mine = lax.dynamic_index_in_dim(blocks, core, 0, keepdims=False)
    other = lax.dynamic_index_in_dim(blocks, 1 - core, 0, keepdims=False)
    other = from_behind(other, "core", 1)
    chip = (mine.astype(jnp.float32) + other.astype(jnp.float32)).astype(jnp.bfloat16)

    dnorm = jnp.dot(dpre, full, preferred_element_type=jnp.float32)
    first = jnp.mean(dnorm, axis=1, keepdims=True)
    second = jnp.mean(dnorm * normed, axis=1, keepdims=True)
    input_grad = (inverse * (dnorm - first - normed * second)).astype(jnp.bfloat16)

    cube = lax.all_to_all(chip, CUBE, 0, 0)
    cube = jnp.sum(cube.astype(jnp.float32), axis=0).astype(jnp.bfloat16)
    group = send_to_all(cube, DATA).reshape(Z_LO, Y, PAD // Z_LO, share)
    total = jnp.sum(group.astype(jnp.float32), axis=1).reshape(PAD, share)[:classes].T
    factor = 1.0 / math.sqrt(total_rows * Z_LO * Y * X * Z_HI * CORE)
    weight_grad = total * (gain32 * factor)
    gain_grad = jnp.sum(weight.astype(jnp.float32) * total, axis=1) * factor
    return (shown, input_grad, weight_grad, gain_grad)


def solution(mesh):
    fine = Mesh(mesh.devices.reshape(Z_LO, Y, X, Z_HI, CORE), NAMES)
    shards = ("x", "z_hi", "core")
    placed = (P(NAMES, None), P(NAMES), P(shards, None), P(shards), P(NAMES), P(NAMES, None))
    return jax.shard_map(
        body,
        mesh=fine,
        in_specs=placed,
        out_specs=(P(NAMES, None), P(NAMES, None), P(shards, None), P(shards)),
        check_vma=False,
    )
```

```python
import math

import jax
import jax.numpy as jnp
from jax import lax
from jax.experimental import pallas as pl
from jax.experimental.pallas import tpu as pltpu
from jax.sharding import Mesh
from jax.sharding import PartitionSpec as P

Z_LO, Y, X, Z_HI, CORE = 2, 8, 8, 4, 2
NAMES = ("z_lo", "y", "x", "z_hi", "core")
DATA = ("z_lo", "y")
PLANE = ("x", "z_hi")
GROUPS, STEP, SHARE = 4, 40, 96
LANES = GROUPS * SHARE
SLOT = 48
INNER = GROUPS * SLOT


def from_behind(value, axes, steps):
    count = lax.axis_size(axes)
    pairs = [(source, (source + steps) % count) for source in range(count)]
    return lax.ppermute(value, axes, pairs)


def vmem_call(kernel, shapes, cost, *operands, scalars=0):
    specs = [
        pl.BlockSpec(memory_space=pltpu.SMEM if place < scalars else pltpu.VMEM)
        for place in range(len(operands))
    ]
    return pl.pallas_call(
        kernel,
        out_shape=shapes,
        in_specs=specs,
        out_specs=[pl.BlockSpec(memory_space=pltpu.VMEM)] * len(shapes),
        compiler_params=pltpu.CompilerParams(vmem_limit_bytes=32 * 1024 * 1024),
        cost_estimate=pl.CostEstimate(flops=cost[0], bytes_accessed=cost[1], transcendentals=0),
    )(*operands)


def prepare_kernel(weight_ref, gain_ref, out_ref):
    classes = weight_ref.shape[0]
    scaled = weight_ref[...].astype(jnp.float32) * gain_ref[...].astype(jnp.float32)
    scaled = jnp.concatenate(
        [scaled, jnp.zeros((GROUPS * STEP - classes, SHARE), jnp.float32)], axis=0
    )
    parts = [scaled[STEP * g : STEP * (g + 1)] for g in range(GROUPS)]
    parcel = jnp.concatenate(parts, axis=1).astype(jnp.bfloat16)
    for place in range(out_ref.shape[0]):
        out_ref[place] = parcel


def main_kernel(
    core_ref, act_ref, own_ref, partner_ref, labels_ref, mask_ref, ids_ref,
    shown_ref, dpre_ref, full_ref, keep_ref, send_ref,
):
    first = core_ref[0] == 0
    count, classes = own_ref.shape[0], shown_ref.shape[1]
    for g in range(GROUPS):
        full_ref[SLOT * g : SLOT * (g + 1)] = jnp.zeros((SLOT, full_ref.shape[1]), jnp.bfloat16)

    for q in range(count // 2):
        shards = []
        for p in (2 * q, 2 * q + 1):
            own, partner = own_ref[p], partner_ref[p]
            shards.append(jnp.where(first, own, partner))
            shards.append(jnp.where(first, partner, own))
        for g in range(GROUPS):
            row = [shard[:, SHARE * g : SHARE * (g + 1)] for shard in shards]
            full_ref[SLOT * g : SLOT * g + STEP, LANES * q : LANES * (q + 1)] = jnp.concatenate(row, axis=1)

    pre = lax.dot_general(
        act_ref[...], full_ref[...], (((1,), (1,)), ((), ())), preferred_element_type=jnp.float32
    )
    ids = ids_ref[...]
    mask = mask_ref[...]
    expo = jnp.where(ids >= 0, jnp.exp(pre), 0.0)
    prob = expo / jnp.sum(expo, axis=1, keepdims=True)
    onehot = jnp.where(labels_ref[...] == ids, 1.0, 0.0)
    dpre32 = 16.0 * (prob - onehot) * mask
    dpre_ref[...] = dpre32.astype(jnp.bfloat16)
    shown = pre * mask
    parts = [shown[:, SLOT * g : SLOT * g + STEP] for g in range(GROUPS)]
    shown_ref[...] = jnp.concatenate(parts, axis=1)[:, :classes].astype(jnp.bfloat16)

    turned = dpre32.T.astype(jnp.bfloat16)
    for q in range(count // 2):
        term = jnp.dot(
            turned, act_ref[:, LANES * q : LANES * (q + 1)], preferred_element_type=jnp.float32
        ).astype(jnp.bfloat16)
        groups = [term[SLOT * g : SLOT * g + STEP] for g in range(GROUPS)]
        shards = [
            jnp.concatenate([group[:, SHARE * k : SHARE * (k + 1)] for group in groups], axis=1)
            for k in range(4)
        ]
        for half in range(2):
            even, odd = shards[2 * half], shards[2 * half + 1]
            keep_ref[2 * q + half] = jnp.where(first, even, odd)
            send_ref[2 * q + half] = jnp.where(first, odd, even)


def move(patches, counts, plan):
    total_rows, width = patches.shape
    slot_count = counts.shape[0]
    patch = total_rows // slot_count
    up, down = plan[0, 0], plan[0, 1]

    def parcel(slot):
        image = lax.dynamic_slice(patches, (slot * patch, 0), (patch, width))
        count = lax.dynamic_slice_in_dim(counts, slot, 1).astype(jnp.bfloat16)
        return jnp.concatenate([image, jnp.broadcast_to(count[:, None], (1, width))])

    arrive_low = from_behind(parcel(up), DATA, 1)
    arrive_up = from_behind(parcel(down), DATA, -1)
    rows = lax.dynamic_update_slice(patches, arrive_low[:patch], (down * patch, 0))
    rows = lax.dynamic_update_slice(rows, arrive_up[:patch], (up * patch, 0))
    slot_ids = jnp.arange(slot_count, dtype=jnp.int32)
    live = jnp.where(
        slot_ids == up,
        arrive_up[patch, 0].astype(jnp.int32),
        jnp.where(slot_ids == down, arrive_low[patch, 0].astype(jnp.int32), counts),
    )
    places = jnp.arange(patch, dtype=jnp.int32)
    mask = (places[None, :] < live[:, None]).astype(jnp.float32).reshape(-1, 1)
    return rows, mask


def body(patches, labels, weight, gain, counts, plan):
    total_rows, width = patches.shape
    share, classes = weight.shape
    peers = X * Z_HI
    core = lax.axis_index("core").astype(jnp.int32)
    wire = jax.ShapeDtypeStruct((peers, STEP, LANES), jnp.bfloat16)
    (copies,) = vmem_call(prepare_kernel, [wire], (0, 2**20), weight.T, gain[None, :])
    plane = lax.all_to_all(copies, PLANE, 0, 0)

    rows, mask = move(patches, counts, plan)
    rows32 = rows.astype(jnp.float32)
    average = jnp.mean(rows32, axis=1, keepdims=True)
    centred = rows32 - average
    inverse = lax.rsqrt(jnp.mean(centred * centred, axis=1, keepdims=True) + 1e-06)
    normed = centred * inverse
    act = normed.astype(jnp.bfloat16)

    partner = from_behind(plane, "core", 1)
    slots = jnp.arange(INNER, dtype=jnp.int32)
    ids = (slots // SLOT) * STEP + slots % SLOT
    ids = jnp.where((slots % SLOT < STEP) & (ids < classes), ids, -1)[None, :]
    shown, dpre, full, keep, send = vmem_call(
        main_kernel,
        [
            jax.ShapeDtypeStruct((total_rows, classes), jnp.bfloat16),
            jax.ShapeDtypeStruct((total_rows, INNER), jnp.bfloat16),
            jax.ShapeDtypeStruct((INNER, width), jnp.bfloat16),
            wire,
            wire,
        ],
        (4 * total_rows * width * INNER, 12 * 2**20),
        core[None], act, plane, partner, labels[:, None], mask, ids,
        scalars=1,
    )
    other = from_behind(send, "core", 1)
    chip = (keep.astype(jnp.float32) + other.astype(jnp.float32)).astype(jnp.bfloat16)

    dnorm = jnp.dot(dpre, full, preferred_element_type=jnp.float32)
    first = jnp.mean(dnorm, axis=1, keepdims=True)
    second = jnp.mean(dnorm * normed, axis=1, keepdims=True)
    input_grad = (inverse * (dnorm - first - normed * second)).astype(jnp.bfloat16)

    owned = lax.all_to_all(chip, PLANE, 0, 0)
    owned = jnp.sum(owned.astype(jnp.float32), axis=0).astype(jnp.bfloat16)
    group = jnp.broadcast_to(owned[None], (Z_LO * Y,) + owned.shape)
    group = lax.all_to_all(group, DATA, 0, 0)
    total = jnp.sum(group.astype(jnp.float32), axis=0)
    total = total.reshape(STEP, GROUPS, share).transpose(1, 0, 2).reshape(GROUPS * STEP, share)
    total = total[:classes]
    factor = 1.0 / math.sqrt(total_rows * Z_LO * Y * X * Z_HI * CORE)
    gain32 = gain.astype(jnp.float32)[None, :]
    weight_grad = (total * (gain32 * factor)).T
    gain_grad = jnp.sum(weight.T.astype(jnp.float32) * total, axis=0) * factor
    return (shown, input_grad, weight_grad, gain_grad)


def solution(mesh):
    fine = Mesh(mesh.devices.reshape(Z_LO, Y, X, Z_HI, CORE), NAMES)
    shards = ("x", "z_hi", "core")
    placed = (P(NAMES, None), P(NAMES), P(shards, None), P(shards), P(NAMES), P(NAMES, None))
    return jax.shard_map(
        body,
        mesh=fine,
        in_specs=placed,
        out_specs=(P(NAMES, None), P(NAMES, None), P(shards, None), P(shards)),
        check_vma=False,
    )
```

```python
import math

import jax
import jax.numpy as jnp
from jax import lax
from jax.experimental import pallas as pl
from jax.experimental.pallas import tpu as pltpu
from jax.sharding import Mesh
from jax.sharding import PartitionSpec as P

Z_LO, Y, X, Z_HI, CORE = 2, 8, 8, 4, 2
NAMES = ("z_lo", "y", "x", "z_hi", "core")
DATA = ("z_lo", "y")
PLANE = ("x", "z_hi")
GROUPS, STEP, SHARE = 4, 40, 96
LANES = GROUPS * SHARE
SLOT = 48
INNER = GROUPS * SLOT


def from_behind(value, axes, steps):
    count = lax.axis_size(axes)
    pairs = [(source, (source + steps) % count) for source in range(count)]
    return lax.ppermute(value, axes, pairs)


def vmem_call(kernel, shapes, cost, *operands, scalars=0, scratch=()):
    specs = [
        pl.BlockSpec(memory_space=pltpu.SMEM if place < scalars else pltpu.VMEM)
        for place in range(len(operands))
    ]
    return pl.pallas_call(
        kernel,
        out_shape=shapes,
        in_specs=specs,
        out_specs=[pl.BlockSpec(memory_space=pltpu.VMEM)] * len(shapes),
        scratch_shapes=list(scratch),
        compiler_params=pltpu.CompilerParams(vmem_limit_bytes=32 * 1024 * 1024),
        cost_estimate=pl.CostEstimate(flops=cost[0], bytes_accessed=cost[1], transcendentals=0),
    )(*operands)


def prepare_kernel(weight_ref, gain_ref, out_ref):
    classes = weight_ref.shape[0]
    scaled = weight_ref[...].astype(jnp.float32) * gain_ref[...].astype(jnp.float32)
    scaled = jnp.concatenate(
        [scaled, jnp.zeros((GROUPS * STEP - classes, SHARE), jnp.float32)], axis=0
    )
    parts = [scaled[STEP * g : STEP * (g + 1)] for g in range(GROUPS)]
    parcel = jnp.concatenate(parts, axis=1).astype(jnp.bfloat16)
    for place in range(out_ref.shape[0]):
        out_ref[place] = parcel


def main_kernel(
    core_ref, act_ref, own_ref, partner_ref, labels_ref, mask_ref, ids_ref,
    shown_ref, dpre_ref, full_ref, keep_ref, send_ref,
):
    first = core_ref[0] == 0
    count, classes = own_ref.shape[0], shown_ref.shape[1]
    for g in range(GROUPS):
        full_ref[SLOT * g : SLOT * (g + 1)] = jnp.zeros((SLOT, full_ref.shape[1]), jnp.bfloat16)

    for q in range(count // 2):
        shards = []
        for p in (2 * q, 2 * q + 1):
            own, partner = own_ref[p], partner_ref[p]
            shards.append(jnp.where(first, own, partner))
            shards.append(jnp.where(first, partner, own))
        for g in range(GROUPS):
            row = [shard[:, SHARE * g : SHARE * (g + 1)] for shard in shards]
            full_ref[SLOT * g : SLOT * g + STEP, LANES * q : LANES * (q + 1)] = jnp.concatenate(row, axis=1)

    pre = lax.dot_general(
        act_ref[...], full_ref[...], (((1,), (1,)), ((), ())), preferred_element_type=jnp.float32
    )
    ids = ids_ref[...]
    mask = mask_ref[...]
    expo = jnp.where(ids >= 0, jnp.exp(pre), 0.0)
    prob = expo / jnp.sum(expo, axis=1, keepdims=True)
    onehot = jnp.where(labels_ref[...] == ids, 1.0, 0.0)
    dpre32 = 16.0 * (prob - onehot) * mask
    dpre_ref[...] = dpre32.astype(jnp.bfloat16)
    shown = pre * mask
    parts = [shown[:, SLOT * g : SLOT * g + STEP] for g in range(GROUPS)]
    shown_ref[...] = jnp.concatenate(parts, axis=1)[:, :classes].astype(jnp.bfloat16)

    turned = dpre32.T.astype(jnp.bfloat16)
    for q in range(count // 2):
        term = jnp.dot(
            turned, act_ref[:, LANES * q : LANES * (q + 1)], preferred_element_type=jnp.float32
        ).astype(jnp.bfloat16)
        groups = [term[SLOT * g : SLOT * g + STEP] for g in range(GROUPS)]
        shards = [
            jnp.concatenate([group[:, SHARE * k : SHARE * (k + 1)] for group in groups], axis=1)
            for k in range(4)
        ]
        for half in range(2):
            even, odd = shards[2 * half], shards[2 * half + 1]
            keep_ref[2 * q + half] = jnp.where(first, even, odd)
            send_ref[2 * q + half] = jnp.where(first, odd, even)


def parcel_kernel(plan_ref, counts_ref, patches_ref, up_ref, down_ref):
    slots = counts_ref.shape[0]
    patch = patches_ref.shape[0] // slots
    for way, out_ref in ((0, up_ref), (1, down_ref)):
        for slot in range(slots):

            @pl.when(plan_ref[0, way] == slot)
            def _(slot=slot, out_ref=out_ref):
                begin = slot * patch // 16 * 16
                end = min(-(-(slot + 1) * patch // 16) * 16, patches_ref.shape[0])
                window = patches_ref[begin:end].astype(jnp.float32)
                image = window[slot * patch - begin : (slot + 1) * patch - begin]
                count = jnp.full((1, image.shape[1]), counts_ref[slot].astype(jnp.float32))
                out_ref[...] = jnp.concatenate([image, count], axis=0).astype(jnp.bfloat16)


def norm_kernel(
    plan_ref, counts_ref, patches_ref, low_ref, high_ref,
    act_ref, inverse_ref, mask_ref, rows_ref,
):
    slots = counts_ref.shape[0]
    total_rows, width = patches_ref.shape
    patch = total_rows // slots
    up, down = plan_ref[0, 0], plan_ref[0, 1]
    rows_ref[...] = patches_ref[...].astype(jnp.float32)
    for slot in range(slots):

        @pl.when(up == slot)
        def _(slot=slot):
            rows_ref[slot * patch : (slot + 1) * patch] = high_ref[:patch].astype(jnp.float32)

        @pl.when(down == slot)
        def _(slot=slot):
            rows_ref[slot * patch : (slot + 1) * patch] = low_ref[:patch].astype(jnp.float32)

    high_live = high_ref[patch : patch + 1, :1].astype(jnp.float32)
    low_live = low_ref[patch : patch + 1, :1].astype(jnp.float32)
    places = lax.broadcasted_iota(jnp.int32, (patch, 1), 0).astype(jnp.float32)
    masks = []
    for slot in range(slots):
        own_live = jnp.full((1, 1), counts_ref[slot].astype(jnp.float32))
        live = jnp.where(up == slot, high_live, jnp.where(down == slot, low_live, own_live))
        masks.append(jnp.where(places < live, 1.0, 0.0))
    mask_ref[...] = jnp.concatenate(masks, axis=0)
    for begin in range(0, total_rows, 16):
        rows = rows_ref[begin : begin + 16]
        centred = rows - jnp.mean(rows, axis=1, keepdims=True)
        inverse = lax.rsqrt(jnp.mean(centred * centred, axis=1, keepdims=True) + 1e-06)
        act_ref[begin : begin + 16] = (centred * inverse).astype(jnp.bfloat16)
        inverse_ref[begin : begin + 16] = inverse


def body(patches, labels, weight, gain, counts, plan):
    total_rows, width = patches.shape
    share, classes = weight.shape
    peers = X * Z_HI
    core = lax.axis_index("core").astype(jnp.int32)
    wire = jax.ShapeDtypeStruct((peers, STEP, LANES), jnp.bfloat16)
    (copies,) = vmem_call(prepare_kernel, [wire], (0, 2**20), weight.T, gain[None, :])
    plane = lax.all_to_all(copies, PLANE, 0, 0)

    image = jax.ShapeDtypeStruct((total_rows // counts.shape[0] + 1, width), jnp.bfloat16)
    column = jax.ShapeDtypeStruct((total_rows, 1), jnp.float32)
    up, down = vmem_call(
        parcel_kernel, [image, image], (0, 3 * 2**20), plan, counts, patches, scalars=2
    )
    arrive_low = from_behind(up, DATA, 1)
    arrive_up = from_behind(down, DATA, -1)
    act, inverse, mask = vmem_call(
        norm_kernel,
        [jax.ShapeDtypeStruct((total_rows, width), jnp.bfloat16), column, column],
        (10 * total_rows * width, 5 * 2**20),
        plan, counts, patches, arrive_low, arrive_up,
        scalars=2,
        scratch=[pltpu.VMEM((total_rows, width), jnp.float32)],
    )

    partner = from_behind(plane, "core", 1)
    slots = jnp.arange(INNER, dtype=jnp.int32)
    ids = (slots // SLOT) * STEP + slots % SLOT
    ids = jnp.where((slots % SLOT < STEP) & (ids < classes), ids, -1)[None, :]
    shown, dpre, full, keep, send = vmem_call(
        main_kernel,
        [
            jax.ShapeDtypeStruct((total_rows, classes), jnp.bfloat16),
            jax.ShapeDtypeStruct((total_rows, INNER), jnp.bfloat16),
            jax.ShapeDtypeStruct((INNER, width), jnp.bfloat16),
            wire,
            wire,
        ],
        (4 * total_rows * width * INNER, 12 * 2**20),
        core[None], act, plane, partner, labels[:, None], mask, ids,
        scalars=1,
    )
    other = from_behind(send, "core", 1)
    chip = (keep.astype(jnp.float32) + other.astype(jnp.float32)).astype(jnp.bfloat16)

    dnorm = jnp.dot(dpre, full, preferred_element_type=jnp.float32)
    first = jnp.mean(dnorm, axis=1, keepdims=True)
    normed = act.astype(jnp.float32)
    second = jnp.mean(dnorm * normed, axis=1, keepdims=True)
    input_grad = (inverse * (dnorm - first - normed * second)).astype(jnp.bfloat16)

    owned = lax.all_to_all(chip, PLANE, 0, 0)
    owned = jnp.sum(owned.astype(jnp.float32), axis=0).astype(jnp.bfloat16)
    group = jnp.broadcast_to(owned[None], (Z_LO * Y,) + owned.shape)
    group = lax.all_to_all(group, DATA, 0, 0)
    total = jnp.sum(group.astype(jnp.float32), axis=0)
    total = total.reshape(STEP, GROUPS, share).transpose(1, 0, 2).reshape(GROUPS * STEP, share)
    total = total[:classes]
    factor = 1.0 / math.sqrt(total_rows * Z_LO * Y * X * Z_HI * CORE)
    gain32 = gain.astype(jnp.float32)[None, :]
    weight_grad = (total * (gain32 * factor)).T
    gain_grad = jnp.sum(weight.T.astype(jnp.float32) * total, axis=0) * factor
    return (shown, input_grad, weight_grad, gain_grad)


def solution(mesh):
    fine = Mesh(mesh.devices.reshape(Z_LO, Y, X, Z_HI, CORE), NAMES)
    shards = ("x", "z_hi", "core")
    placed = (P(NAMES, None), P(NAMES), P(shards, None), P(shards), P(NAMES), P(NAMES, None))
    return jax.shard_map(
        body,
        mesh=fine,
        in_specs=placed,
        out_specs=(P(NAMES, None), P(NAMES, None), P(shards, None), P(shards)),
        check_vma=False,
    )
```

```python
import functools
import math

import jax
import jax.numpy as jnp
from jax import lax
from jax.experimental import pallas as pl
from jax.experimental.pallas import tpu as pltpu
from jax.sharding import Mesh
from jax.sharding import PartitionSpec as P

Z_LO, Y, X, Z_HI, CORE = 2, 8, 8, 4, 2
NAMES = ("z_lo", "y", "x", "z_hi", "core")
DATA = ("z_lo", "y")
PLANE = ("x", "z_hi")
CUBE = ("z_lo", "x", "z_hi")
GROUPS, STEP, SHARE = 4, 40, 96
LANES = GROUPS * SHARE
SLOT = 48
INNER = GROUPS * SLOT
HALVES, CUT, TAIL = 2, 16, 24


def from_behind(value, axes, steps):
    count = lax.axis_size(axes)
    pairs = [(source, (source + steps) % count) for source in range(count)]
    return lax.ppermute(value, axes, pairs)


def vmem_call(kernel, shapes, cost, *operands, mib, scalars=0, scratch=()):
    specs = [
        pl.BlockSpec(memory_space=pltpu.SMEM if place < scalars else pltpu.VMEM)
        for place in range(len(operands))
    ]
    return pl.pallas_call(
        kernel,
        out_shape=shapes,
        in_specs=specs,
        out_specs=[pl.BlockSpec(memory_space=pltpu.VMEM)] * len(shapes),
        scratch_shapes=list(scratch),
        compiler_params=pltpu.CompilerParams(vmem_limit_bytes=mib * 2**20),
        cost_estimate=pl.CostEstimate(flops=cost[0], bytes_accessed=cost[1], transcendentals=0),
    )(*operands)


def prepare_kernel(weight_ref, gain_ref, out_ref):
    classes = weight_ref.shape[0]
    scaled = weight_ref[...].astype(jnp.float32) * gain_ref[...].astype(jnp.float32)
    scaled = jnp.concatenate(
        [scaled, jnp.zeros((GROUPS * STEP - classes, SHARE), jnp.float32)], axis=0
    )
    parts = [scaled[STEP * g : STEP * (g + 1)] for g in range(GROUPS)]
    parcel = jnp.concatenate(parts, axis=1).astype(jnp.bfloat16)
    for place in range(out_ref.shape[0]):
        out_ref[place] = parcel


def unpack(core_ref, own_ref, partner_ref, full_ref):
    first = core_ref[0] == 0
    for g in range(GROUPS):
        full_ref[SLOT * g : SLOT * (g + 1)] = jnp.zeros((SLOT, full_ref.shape[1]), jnp.bfloat16)
    for q in range(own_ref.shape[0] // 2):
        shards = []
        for p in (2 * q, 2 * q + 1):
            own, partner = own_ref[p], partner_ref[p]
            shards.append(jnp.where(first, own, partner))
            shards.append(jnp.where(first, partner, own))
        for g in range(GROUPS):
            row = [shard[:, SHARE * g : SHARE * (g + 1)] for shard in shards]
            full_ref[SLOT * g : SLOT * g + STEP, LANES * q : LANES * (q + 1)] = jnp.concatenate(row, axis=1)


def main_kernel(
    core_ref, act_ref, own_ref, partner_ref, labels_ref, mask_ref, ids_ref,
    shown_ref, dpre_ref, keep_ref, send_ref, full_ref,
):
    first = core_ref[0] == 0
    count, classes = own_ref.shape[0], shown_ref.shape[1]
    unpack(core_ref, own_ref, partner_ref, full_ref)
    pre = lax.dot_general(
        act_ref[...], full_ref[...], (((1,), (1,)), ((), ())), preferred_element_type=jnp.float32
    )
    ids = ids_ref[...]
    mask = mask_ref[...]
    expo = jnp.where(ids >= 0, jnp.exp(pre), 0.0)
    prob = expo / jnp.sum(expo, axis=1, keepdims=True)
    onehot = jnp.where(labels_ref[...] == ids, 1.0, 0.0)
    dpre32 = 16.0 * (prob - onehot) * mask
    dpre_ref[...] = dpre32.astype(jnp.bfloat16)
    shown = pre * mask
    parts = [shown[:, SLOT * g : SLOT * g + STEP] for g in range(GROUPS)]
    shown_ref[...] = jnp.concatenate(parts, axis=1)[:, :classes].astype(jnp.bfloat16)

    turned = dpre32.T.astype(jnp.bfloat16)
    for q in range(count // 2):
        term = jnp.dot(
            turned, act_ref[:, LANES * q : LANES * (q + 1)], preferred_element_type=jnp.float32
        ).astype(jnp.bfloat16)
        groups = [term[SLOT * g : SLOT * g + STEP] for g in range(GROUPS)]
        for half in range(HALVES):
            shards = []
            for k in range(4):
                lanes = [groups[2 * half + g][:, SHARE * k : SHARE * (k + 1)] for g in range(2)]
                lanes = jnp.concatenate(lanes, axis=1)
                tail = lanes[:, 128:]
                left = tail[CUT:]
                right = jnp.concatenate([tail[:CUT], jnp.zeros((TAIL - CUT, 64), jnp.bfloat16)], axis=0)
                shards.append((lanes[:, :128], jnp.concatenate([left, right], axis=1)))
            for pair in range(2):
                even, odd = shards[2 * pair], shards[2 * pair + 1]
                place = 2 * q + pair
                for rows, e, o in ((slice(0, STEP), even[0], odd[0]), (slice(STEP, STEP + TAIL), even[1], odd[1])):
                    keep_ref[half, place, rows] = jnp.where(first, e, o)
                    send_ref[half, place, rows] = jnp.where(first, o, e)


def input_kernel(
    core_ref, act_ref, own_ref, partner_ref, dpre_ref, inverse_ref,
    out_ref, full_ref, dnorm_ref,
):
    unpack(core_ref, own_ref, partner_ref, full_ref)
    dpre = dpre_ref[...]
    width = act_ref.shape[1]
    tiles = [slice(begin, begin + LANES) for begin in range(0, width, LANES)]
    first = second = 0.0
    for tile in tiles:
        dnorm = jnp.dot(dpre, full_ref[:, tile], preferred_element_type=jnp.float32)
        dnorm_ref[:, tile] = dnorm
        first += jnp.sum(dnorm, axis=1, keepdims=True)
        second += jnp.sum(dnorm * act_ref[:, tile].astype(jnp.float32), axis=1, keepdims=True)
    inverse = inverse_ref[...]
    first = first * (1.0 / width)
    second = second * (1.0 / width)
    for tile in tiles:
        inner = dnorm_ref[:, tile] - first - act_ref[:, tile].astype(jnp.float32) * second
        out_ref[:, tile] = (inverse * inner).astype(jnp.bfloat16)


def final_kernel(group_ref, weight_ref, gain_ref, weight_grad_ref, gain_grad_ref, *, factor):
    classes = weight_ref.shape[0]
    members = group_ref.shape[0] // HALVES
    parts = []
    for half in range(HALVES):
        total = group_ref[half * members].astype(jnp.float32)
        for member in range(1, members):
            total += group_ref[half * members + member].astype(jnp.float32)
        packed = total[STEP:]
        tail = jnp.concatenate([packed[:CUT, 64:], packed[: STEP - CUT, :64]], axis=0)
        lanes = jnp.concatenate([total[:STEP], tail], axis=1)
        parts += [lanes[:, :SHARE], lanes[:, SHARE:]]
    total = jnp.concatenate(parts, axis=0)[:classes] * factor
    weight_grad_ref[...] = total * gain_ref[...].astype(jnp.float32)
    product = total * weight_ref[...].astype(jnp.float32)
    gain_grad_ref[...] = jnp.sum(product, axis=0, keepdims=True)


def parcel_kernel(plan_ref, counts_ref, patches_ref, up_ref, down_ref):
    slots = counts_ref.shape[0]
    patch = patches_ref.shape[0] // slots
    for way, out_ref in ((0, up_ref), (1, down_ref)):
        for slot in range(slots):

            @pl.when(plan_ref[0, way] == slot)
            def _(slot=slot, out_ref=out_ref):
                begin = slot * patch // 16 * 16
                end = min(-(-(slot + 1) * patch // 16) * 16, patches_ref.shape[0])
                window = patches_ref[begin:end].astype(jnp.float32)
                image = window[slot * patch - begin : (slot + 1) * patch - begin]
                count = jnp.full((1, image.shape[1]), counts_ref[slot].astype(jnp.float32))
                out_ref[...] = jnp.concatenate([image, count], axis=0).astype(jnp.bfloat16)


def norm_kernel(
    plan_ref, counts_ref, patches_ref, low_ref, high_ref,
    act_ref, inverse_ref, mask_ref, rows_ref,
):
    slots = counts_ref.shape[0]
    total_rows, width = patches_ref.shape
    patch = total_rows // slots
    up, down = plan_ref[0, 0], plan_ref[0, 1]
    rows_ref[...] = patches_ref[...].astype(jnp.float32)
    for slot in range(slots):

        @pl.when(up == slot)
        def _(slot=slot):
            rows_ref[slot * patch : (slot + 1) * patch] = high_ref[:patch].astype(jnp.float32)

        @pl.when(down == slot)
        def _(slot=slot):
            rows_ref[slot * patch : (slot + 1) * patch] = low_ref[:patch].astype(jnp.float32)

    high_live = high_ref[patch : patch + 1, :1].astype(jnp.float32)
    low_live = low_ref[patch : patch + 1, :1].astype(jnp.float32)
    places = lax.broadcasted_iota(jnp.int32, (patch, 1), 0).astype(jnp.float32)
    masks = []
    for slot in range(slots):
        own_live = jnp.full((1, 1), counts_ref[slot].astype(jnp.float32))
        live = jnp.where(up == slot, high_live, jnp.where(down == slot, low_live, own_live))
        masks.append(jnp.where(places < live, 1.0, 0.0))
    mask_ref[...] = jnp.concatenate(masks, axis=0)
    for begin in range(0, total_rows, 16):
        rows = rows_ref[begin : begin + 16]
        centred = rows - jnp.mean(rows, axis=1, keepdims=True)
        inverse = lax.rsqrt(jnp.mean(centred * centred, axis=1, keepdims=True) + 1e-06)
        act_ref[begin : begin + 16] = (centred * inverse).astype(jnp.bfloat16)
        inverse_ref[begin : begin + 16] = inverse


def body(patches, labels, weight, gain, counts, plan):
    total_rows, width = patches.shape
    share, classes = weight.shape
    peers = X * Z_HI
    core = lax.axis_index("core").astype(jnp.int32)
    wire = jax.ShapeDtypeStruct((peers, STEP, LANES), jnp.bfloat16)
    (copies,) = vmem_call(
        prepare_kernel, [wire], (0, 2**20), weight.T, gain[None, :], mib=4
    )
    plane = lax.all_to_all(copies, PLANE, 0, 0)

    image = jax.ShapeDtypeStruct((total_rows // counts.shape[0] + 1, width), jnp.bfloat16)
    column = jax.ShapeDtypeStruct((total_rows, 1), jnp.float32)
    up, down = vmem_call(
        parcel_kernel, [image, image], (0, 3 * 2**20), plan, counts, patches, mib=6, scalars=2
    )
    arrive_low = from_behind(up, DATA, 1)
    arrive_up = from_behind(down, DATA, -1)
    act, inverse, mask = vmem_call(
        norm_kernel,
        [jax.ShapeDtypeStruct((total_rows, width), jnp.bfloat16), column, column],
        (10 * total_rows * width, 5 * 2**20),
        plan, counts, patches, arrive_low, arrive_up,
        mib=14,
        scalars=2,
        scratch=[pltpu.VMEM((total_rows, width), jnp.float32)],
    )

    plane, inverse = lax.optimization_barrier((plane, inverse))
    partner = from_behind(plane, "core", 1)
    slots = jnp.arange(INNER, dtype=jnp.int32)
    ids = (slots // SLOT) * STEP + slots % SLOT
    ids = jnp.where((slots % SLOT < STEP) & (ids < classes), ids, -1)[None, :]
    halves = jax.ShapeDtypeStruct((HALVES, peers, STEP + TAIL, 128), jnp.bfloat16)
    full = pltpu.VMEM((INNER, width), jnp.bfloat16)
    shown, dpre, keep, send = vmem_call(
        main_kernel,
        [
            jax.ShapeDtypeStruct((total_rows, classes), jnp.bfloat16),
            jax.ShapeDtypeStruct((total_rows, INNER), jnp.bfloat16),
            halves,
            halves,
        ],
        (4 * total_rows * width * INNER, 8 * 2**20),
        core[None], act, plane, partner, labels[:, None], mask, ids,
        mib=20,
        scalars=1,
        scratch=[full],
    )
    other = from_behind(send, "core", 1)
    chip = (keep.astype(jnp.float32) + other.astype(jnp.float32)).astype(jnp.bfloat16)
    chip, dpre = lax.optimization_barrier((chip, dpre))
    (input_grad,) = vmem_call(
        input_kernel,
        [jax.ShapeDtypeStruct((total_rows, width), jnp.bfloat16)],
        (2 * total_rows * width * INNER, 6 * 2**20),
        core[None], act, plane, partner, dpre, inverse,
        mib=20,
        scalars=1,
        scratch=[full, pltpu.VMEM((total_rows, width), jnp.float32)],
    )

    owned = lax.all_to_all(chip.reshape(HALVES * peers, STEP + TAIL, 128), CUBE, 0, 0)
    owned, input_grad = lax.optimization_barrier((owned, input_grad))
    owned = jnp.sum(owned.astype(jnp.float32), axis=0).astype(jnp.bfloat16)
    group = jnp.broadcast_to(owned[None], (Z_LO * Y,) + owned.shape)
    group = lax.all_to_all(group, DATA, 0, 0)
    factor = 1.0 / math.sqrt(total_rows * Z_LO * Y * X * Z_HI * CORE)
    weight_grad, gain_grad = vmem_call(
        functools.partial(final_kernel, factor=factor),
        [
            jax.ShapeDtypeStruct((classes, share), jnp.float32),
            jax.ShapeDtypeStruct((1, share), jnp.float32),
        ],
        (0, 2**20),
        group, weight.T, gain[None, :],
        mib=4,
    )
    return (shown, input_grad, weight_grad.T, gain_grad[0])


def solution(mesh):
    fine = Mesh(mesh.devices.reshape(Z_LO, Y, X, Z_HI, CORE), NAMES)
    shards = ("x", "z_hi", "core")
    placed = (P(NAMES, None), P(NAMES), P(shards, None), P(shards), P(NAMES), P(NAMES, None))
    return jax.shard_map(
        body,
        mesh=fine,
        in_specs=placed,
        out_specs=(P(NAMES, None), P(NAMES, None), P(shards, None), P(shards)),
        check_vma=False,
    )
```

```python
import functools
import math

import jax
import jax.numpy as jnp
from jax import lax
from jax.experimental import pallas as pl
from jax.experimental.pallas import tpu as pltpu
from jax.sharding import Mesh
from jax.sharding import PartitionSpec as P

Z_LO, Y, X, Z_HI, CORE = 2, 8, 8, 4, 2
NAMES = ("z_lo", "y", "x", "z_hi", "core")
DATA = ("z_lo", "y")
PLANE = ("x", "z_hi")
CUBE = ("z_lo", "x", "z_hi")
GROUPS, STEP, SHARE = 4, 40, 96
LANES = GROUPS * SHARE
SLOT = 48
INNER = GROUPS * SLOT
HALVES, CUT, TAIL = 2, 16, 24


def from_behind(value, axes, steps):
    count = lax.axis_size(axes)
    pairs = [(source, (source + steps) % count) for source in range(count)]
    return lax.ppermute(value, axes, pairs)


def vmem_call(kernel, shapes, cost, *operands, mib, scalars=0, scratch=()):
    specs = [
        pl.BlockSpec(memory_space=pltpu.SMEM if place < scalars else pltpu.VMEM)
        for place in range(len(operands))
    ]
    return pl.pallas_call(
        kernel,
        out_shape=shapes,
        in_specs=specs,
        out_specs=[pl.BlockSpec(memory_space=pltpu.VMEM)] * len(shapes),
        scratch_shapes=list(scratch),
        compiler_params=pltpu.CompilerParams(vmem_limit_bytes=mib * 2**20),
        cost_estimate=pl.CostEstimate(flops=cost[0], bytes_accessed=cost[1], transcendentals=0),
    )(*operands)


def prepare_kernel(weight_ref, gain_ref, out_ref):
    classes = weight_ref.shape[0]
    scaled = weight_ref[...].astype(jnp.float32) * gain_ref[...].astype(jnp.float32)
    scaled = jnp.concatenate(
        [scaled, jnp.zeros((GROUPS * STEP - classes, SHARE), jnp.float32)], axis=0
    )
    parts = [scaled[STEP * g : STEP * (g + 1)] for g in range(GROUPS)]
    parcel = jnp.concatenate(parts, axis=1).astype(jnp.bfloat16)
    for place in range(out_ref.shape[0]):
        out_ref[place] = parcel


def unpack(core_ref, own_ref, partner_ref, full_ref):
    first = core_ref[0] == 0
    for g in range(GROUPS):
        full_ref[SLOT * g : SLOT * (g + 1)] = jnp.zeros((SLOT, full_ref.shape[1]), jnp.bfloat16)
    for q in range(own_ref.shape[0] // 2):
        shards = []
        for p in (2 * q, 2 * q + 1):
            own, partner = own_ref[p], partner_ref[p]
            shards.append(jnp.where(first, own, partner))
            shards.append(jnp.where(first, partner, own))
        for g in range(GROUPS):
            row = [shard[:, SHARE * g : SHARE * (g + 1)] for shard in shards]
            full_ref[SLOT * g : SLOT * g + STEP, LANES * q : LANES * (q + 1)] = jnp.concatenate(row, axis=1)


def main_kernel(
    core_ref, act_ref, own_ref, partner_ref, labels_ref, mask_ref, ids_ref,
    shown_ref, dpre_ref, keep_ref, send_ref, full_ref,
):
    first = core_ref[0] == 0
    count, classes = own_ref.shape[0], shown_ref.shape[1]
    unpack(core_ref, own_ref, partner_ref, full_ref)
    pre = lax.dot_general(
        act_ref[...], full_ref[...], (((1,), (1,)), ((), ())), preferred_element_type=jnp.float32
    )
    ids = ids_ref[...]
    mask = mask_ref[...]
    expo = jnp.where(ids >= 0, jnp.exp(pre), 0.0)
    prob = expo / jnp.sum(expo, axis=1, keepdims=True)
    onehot = jnp.where(labels_ref[...] == ids, 1.0, 0.0)
    dpre32 = 16.0 * (prob - onehot) * mask
    dpre_ref[...] = dpre32.astype(jnp.bfloat16)
    shown = pre * mask
    parts = [shown[:, SLOT * g : SLOT * g + STEP] for g in range(GROUPS)]
    shown_ref[...] = jnp.concatenate(parts, axis=1)[:, :classes].astype(jnp.bfloat16)

    turned = dpre32.T.astype(jnp.bfloat16)
    for q in range(count // 2):
        term = jnp.dot(
            turned, act_ref[:, LANES * q : LANES * (q + 1)], preferred_element_type=jnp.float32
        ).astype(jnp.bfloat16)
        groups = [term[SLOT * g : SLOT * g + STEP] for g in range(GROUPS)]
        for half in range(HALVES):
            shards = []
            for k in range(4):
                lanes = [groups[2 * half + g][:, SHARE * k : SHARE * (k + 1)] for g in range(2)]
                lanes = jnp.concatenate(lanes, axis=1)
                tail = lanes[:, 128:]
                left = tail[CUT:]
                right = jnp.concatenate([tail[:CUT], jnp.zeros((TAIL - CUT, 64), jnp.bfloat16)], axis=0)
                shards.append((lanes[:, :128], jnp.concatenate([left, right], axis=1)))
            for pair in range(2):
                even, odd = shards[2 * pair], shards[2 * pair + 1]
                place = 2 * q + pair
                for rows, e, o in ((slice(0, STEP), even[0], odd[0]), (slice(STEP, STEP + TAIL), even[1], odd[1])):
                    keep_ref[half, place, rows] = jnp.where(first, e, o)
                    send_ref[half, place, rows] = jnp.where(first, o, e)


def input_kernel(
    core_ref, act_ref, own_ref, partner_ref, dpre_ref, inverse_ref,
    out_ref, full_ref, dnorm_ref,
):
    unpack(core_ref, own_ref, partner_ref, full_ref)
    dpre = dpre_ref[...]
    width = act_ref.shape[1]
    tiles = [slice(begin, begin + LANES) for begin in range(0, width, LANES)]
    first = second = 0.0
    for tile in tiles:
        dnorm = jnp.dot(dpre, full_ref[:, tile], preferred_element_type=jnp.float32)
        dnorm_ref[:, tile] = dnorm
        first += jnp.sum(dnorm, axis=1, keepdims=True)
        second += jnp.sum(dnorm * act_ref[:, tile].astype(jnp.float32), axis=1, keepdims=True)
    inverse = inverse_ref[...]
    first = first * (1.0 / width)
    second = second * (1.0 / width)
    for tile in tiles:
        inner = dnorm_ref[:, tile] - first - act_ref[:, tile].astype(jnp.float32) * second
        out_ref[:, tile] = (inverse * inner).astype(jnp.bfloat16)


def final_kernel(group_ref, weight_ref, gain_ref, weight_grad_ref, gain_grad_ref, *, factor):
    classes = weight_ref.shape[0]
    members = group_ref.shape[0] // HALVES
    parts = []
    for half in range(HALVES):
        total = group_ref[half * members].astype(jnp.float32)
        for member in range(1, members):
            total += group_ref[half * members + member].astype(jnp.float32)
        packed = total[STEP:]
        tail = jnp.concatenate([packed[:CUT, 64:], packed[: STEP - CUT, :64]], axis=0)
        lanes = jnp.concatenate([total[:STEP], tail], axis=1)
        parts += [lanes[:, :SHARE], lanes[:, SHARE:]]
    total = jnp.concatenate(parts, axis=0)[:classes] * factor
    weight_grad_ref[...] = total * gain_ref[...].astype(jnp.float32)
    product = total * weight_ref[...].astype(jnp.float32)
    gain_grad_ref[...] = jnp.sum(product, axis=0, keepdims=True)


def parcel_kernel(plan_ref, counts_ref, patches_ref, up_ref, down_ref):
    slots = counts_ref.shape[0]
    patch = patches_ref.shape[0] // slots
    for way, out_ref in ((0, up_ref), (1, down_ref)):
        for slot in range(slots):

            @pl.when(plan_ref[0, way] == slot)
            def _(slot=slot, out_ref=out_ref):
                begin = slot * patch // 16 * 16
                end = min(-(-(slot + 1) * patch // 16) * 16, patches_ref.shape[0])
                window = patches_ref[begin:end].astype(jnp.float32)
                image = window[slot * patch - begin : (slot + 1) * patch - begin]
                count = jnp.full((1, image.shape[1]), counts_ref[slot].astype(jnp.float32))
                out_ref[...] = jnp.concatenate([image, count], axis=0).astype(jnp.bfloat16)


def norm_kernel(
    plan_ref, counts_ref, patches_ref, low_ref, high_ref,
    act_ref, inverse_ref, mask_ref, rows_ref,
):
    slots = counts_ref.shape[0]
    total_rows, width = patches_ref.shape
    patch = total_rows // slots
    up, down = plan_ref[0, 0], plan_ref[0, 1]
    rows_ref[...] = patches_ref[...].astype(jnp.float32)
    for slot in range(slots):

        @pl.when(up == slot)
        def _(slot=slot):
            rows_ref[slot * patch : (slot + 1) * patch] = high_ref[:patch].astype(jnp.float32)

        @pl.when(down == slot)
        def _(slot=slot):
            rows_ref[slot * patch : (slot + 1) * patch] = low_ref[:patch].astype(jnp.float32)

    high_live = high_ref[patch : patch + 1, :1].astype(jnp.float32)
    low_live = low_ref[patch : patch + 1, :1].astype(jnp.float32)
    places = lax.broadcasted_iota(jnp.int32, (patch, 1), 0).astype(jnp.float32)
    masks = []
    for slot in range(slots):
        own_live = jnp.full((1, 1), counts_ref[slot].astype(jnp.float32))
        live = jnp.where(up == slot, high_live, jnp.where(down == slot, low_live, own_live))
        masks.append(jnp.where(places < live, 1.0, 0.0))
    mask_ref[...] = jnp.concatenate(masks, axis=0)
    for begin in range(0, total_rows, 16):
        rows = rows_ref[begin : begin + 16]
        centred = rows - jnp.mean(rows, axis=1, keepdims=True)
        inverse = lax.rsqrt(jnp.mean(centred * centred, axis=1, keepdims=True) + 1e-06)
        act_ref[begin : begin + 16] = (centred * inverse).astype(jnp.bfloat16)
        inverse_ref[begin : begin + 16] = inverse


def body(patches, labels, weight, gain, counts, plan):
    total_rows, width = patches.shape
    share, classes = weight.shape
    peers = X * Z_HI
    core = lax.axis_index("core").astype(jnp.int32)
    wire = jax.ShapeDtypeStruct((peers, STEP, LANES), jnp.bfloat16)
    (copies,) = vmem_call(
        prepare_kernel, [wire], (0, 2**20), weight.T, gain[None, :], mib=4
    )
    plane = lax.all_to_all(copies, PLANE, 0, 0)

    image = jax.ShapeDtypeStruct((total_rows // counts.shape[0] + 1, width), jnp.bfloat16)
    column = jax.ShapeDtypeStruct((total_rows, 1), jnp.float32)
    up, down = vmem_call(
        parcel_kernel, [image, image], (0, 3 * 2**20), plan, counts, patches, mib=6, scalars=2
    )
    arrive_low = from_behind(up, DATA, 1)
    arrive_up = from_behind(down, DATA, -1)
    act, inverse, mask = vmem_call(
        norm_kernel,
        [jax.ShapeDtypeStruct((total_rows, width), jnp.bfloat16), column, column],
        (2**37, 5 * 2**20),
        plan, counts, patches, arrive_low, arrive_up,
        mib=14,
        scalars=2,
        scratch=[pltpu.VMEM((total_rows, width), jnp.float32)],
    )

    plane, inverse = lax.optimization_barrier((plane, inverse))
    partner = from_behind(plane, "core", 1)
    slots = jnp.arange(INNER, dtype=jnp.int32)
    ids = (slots // SLOT) * STEP + slots % SLOT
    ids = jnp.where((slots % SLOT < STEP) & (ids < classes), ids, -1)[None, :]
    halves = jax.ShapeDtypeStruct((HALVES, peers, STEP + TAIL, 128), jnp.bfloat16)
    full = pltpu.VMEM((INNER, width), jnp.bfloat16)
    shown, dpre, keep, send = vmem_call(
        main_kernel,
        [
            jax.ShapeDtypeStruct((total_rows, classes), jnp.bfloat16),
            jax.ShapeDtypeStruct((total_rows, INNER), jnp.bfloat16),
            halves,
            halves,
        ],
        (4 * total_rows * width * INNER, 8 * 2**20),
        core[None], act, plane, partner, labels[:, None], mask, ids,
        mib=20,
        scalars=1,
        scratch=[full],
    )
    other = from_behind(send, "core", 1)
    chip = (keep.astype(jnp.float32) + other.astype(jnp.float32)).astype(jnp.bfloat16)
    chip, dpre = lax.optimization_barrier((chip, dpre))
    (input_grad,) = vmem_call(
        input_kernel,
        [jax.ShapeDtypeStruct((total_rows, width), jnp.bfloat16)],
        (2 * total_rows * width * INNER, 6 * 2**20),
        core[None], act, plane, partner, dpre, inverse,
        mib=20,
        scalars=1,
        scratch=[full, pltpu.VMEM((total_rows, width), jnp.float32)],
    )

    owned = lax.all_to_all(chip.reshape(HALVES * peers, STEP + TAIL, 128), CUBE, 0, 0)
    owned, input_grad = lax.optimization_barrier((owned, input_grad))
    owned = jnp.sum(owned.astype(jnp.float32), axis=0).astype(jnp.bfloat16)
    group = jnp.broadcast_to(owned[None], (Z_LO * Y,) + owned.shape)
    group = lax.all_to_all(group, DATA, 0, 0)
    factor = 1.0 / math.sqrt(total_rows * Z_LO * Y * X * Z_HI * CORE)
    weight_grad, gain_grad = vmem_call(
        functools.partial(final_kernel, factor=factor),
        [
            jax.ShapeDtypeStruct((classes, share), jnp.float32),
            jax.ShapeDtypeStruct((1, share), jnp.float32),
        ],
        (0, 2**20),
        group, weight.T, gain[None, :],
        mib=4,
    )
    return (shown, input_grad, weight_grad.T, gain_grad[0])


def solution(mesh):
    fine = Mesh(mesh.devices.reshape(Z_LO, Y, X, Z_HI, CORE), NAMES)
    shards = ("x", "z_hi", "core")
    placed = (P(NAMES, None), P(NAMES), P(shards, None), P(shards), P(NAMES), P(NAMES, None))
    return jax.shard_map(
        body,
        mesh=fine,
        in_specs=placed,
        out_specs=(P(NAMES, None), P(NAMES, None), P(shards, None), P(shards)),
        check_vma=False,
    )
```
